256 devices in a mesh: dp: 16 (over x_hi, z), mp: 16 (over x_lo, y, core).
Axes of the slice: x: 4 (x_hi: 2, x_lo: 2; x = x_hi * 2 + x_lo), y: 4, z: 8, core: 2. Of those that a mesh axis runs over, the one named last changes fastest.
Arguments:
- inputs: bfloat16 [6144, 4096], P('dp', 'mp'), may hold values from -6 to 6
- out_cotangent: bfloat16 [6144, 4096], P('dp'), may hold values from -6 to 6
- gate_weight: bfloat16 [4096, 6144], P('dp', 'mp'), may hold values from -0.09375 to 0.09375
- linear_weight: bfloat16 [4096, 6144], P('dp', 'mp'), may hold values from -0.09375 to 0.09375
- output_weight: bfloat16 [6144, 4096], P('mp', 'dp'), may hold values from -0.078125 to 0.078125
Outputs:
- layer_output: bfloat16 [6144, 4096], P('dp', 'mp')
- input_grad: bfloat16 [6144, 4096], P('dp', 'mp')
- gate_grad: float32 [4096, 6144], P('dp', 'mp')
- linear_grad: float32 [4096, 6144], P('dp', 'mp')
- output_grad: float32 [6144, 4096], P('mp', 'dp')
The draws below stay inside these ranges and needn't reach their ends.
All inputs are finite; a program needn't handle non-finite values.
Results may differ from the reference program's by a relative error of at most 0.023.
Values may be sent and summed in bfloat16 or wider, within the bound.
No kernel may reach another device: no remote copies, remote signals or barrier semaphores. Data moves between devices by JAX's collectives and lax.ppermute only.
A program may use at most 128 MiB of HBM per device.

```python
import jax
import jax.numpy as jnp
from jax import lax

D = 4096
FF = 6144
TOK_DEV = 384
TOKENS = 6144
N_DP = 16
N_MP = 16


def raised(entries, rng, source, target, blocks, factor):
    owner, partner = [(jnp.arange(entries.shape[position]) // (entries.shape[position] // blocks)).reshape([-1 if axis == position else 1 for axis in range(entries.ndim)]) for position in (source, target)]
    chosen = jax.random.permutation(rng, blocks)[partner]
    strong = (owner == chosen) | (owner == (partner + blocks // 2) % blocks)
    return jnp.where(strong, factor * entries, entries)


def steps_of(stream_key, dims, split, smallest, top_value):
    def one(dim, shards_of):
        steps = jax.random.uniform(jax.random.fold_in(jax.random.fold_in(stream_key, 6), dim), (shards_of,), jnp.float32, smallest / len(split), top_value / len(split))
        return jnp.repeat(jnp.exp(steps), dims[dim] // shards_of).reshape((-1,) + (1,) * (len(dims) - dim - 1))

    level = one(*split[0])
    for cut in split[1:]:
        level = level * one(*cut)
    return level


def gaussian(own_key, dims, deviation, limit, pieces=(), kind=jnp.bfloat16):
    factor_of = steps_of(own_key, dims, pieces, -0.22, 0.18) if pieces else 1.0
    result = jax.random.normal(own_key, dims, jnp.float32) * deviation * factor_of
    return jnp.minimum(jnp.maximum(result, -limit), limit).astype(kind)


def noise_with(stream_key, extent, scale, reach, split, heavy, kind=jnp.bfloat16):
    values = scale * jax.random.normal(stream_key, extent, jnp.float32)
    if split:
        values = values * steps_of(stream_key, extent, split, -0.22, 0.18)
    return jnp.clip(raised(values, jax.random.fold_in(stream_key, 3), *heavy), -reach, reach).astype(kind)


def setup_inputs(seed: int = 0) -> dict:
    streams_of = jax.random.split(jax.random.key(seed), 6)
    inputs = noise_with(streams_of[0], (TOKENS, D), 1.0, 6.0, ((0, 16), (1, 16)), (0, 1, 16, 2.0))
    out_cotangent = noise_with(streams_of[1], (TOKENS, D), 1.0, 6.0, ((0, 16),), (0, 1, 16, 2.0))
    gate_weight = gaussian(streams_of[2], (D, FF), D ** -0.5, 0.09375, ((0, 16), (1, 16)))
    linear_weight = gaussian(streams_of[3], (D, FF), D ** -0.5, 0.09375, ((0, 16), (1, 16)))
    output_weight = gaussian(streams_of[4], (FF, D), FF ** -0.5, 0.078125, ((0, 16), (1, 16)))
    return dict(inputs=inputs, out_cotangent=out_cotangent, gate_weight=gate_weight, linear_weight=linear_weight, output_weight=output_weight)


def gelu_tanh(values):
    return jax.nn.gelu(values, approximate=True)

def reference(inputs, out_cotangent, gate_weight, linear_weight, output_weight):
    gate = jnp.dot(inputs, gate_weight, preferred_element_type=jnp.float32)
    linear = jnp.dot(inputs, linear_weight, preferred_element_type=jnp.float32)
    activated, gelu_back = jax.vjp(gelu_tanh, gate)
    hidden = (activated * linear).astype(jnp.bfloat16)
    width = FF // N_MP
    hidden_blocks = hidden.reshape(TOKENS, N_MP, width).transpose(1, 0, 2)
    out_blocks = output_weight.reshape(N_MP, width, D)

    def out_step(total, pair):
        part = jnp.dot(pair[0], pair[1], preferred_element_type=jnp.float32).astype(jnp.bfloat16)
        return (total + part.astype(jnp.float32), None)
    layer_output, _ = lax.scan(out_step, jnp.zeros((TOKENS, D), jnp.float32), (hidden_blocks, out_blocks))
    hidden_cot = jnp.dot(out_cotangent, output_weight.T, preferred_element_type=jnp.float32)
    gate_cot = gelu_back(hidden_cot * linear)[0].astype(jnp.bfloat16)
    linear_cot = (hidden_cot * activated).astype(jnp.bfloat16)
    gate_cb = gate_cot.reshape(TOKENS, N_MP, width).transpose(1, 0, 2)
    linear_cb = linear_cot.reshape(TOKENS, N_MP, width).transpose(1, 0, 2)
    gate_wb = gate_weight.reshape(D, N_MP, width).transpose(1, 0, 2)
    linear_wb = linear_weight.reshape(D, N_MP, width).transpose(1, 0, 2)

    def in_step(total, items):
        part = jnp.dot(items[0], items[2].T, preferred_element_type=jnp.float32)
        part = part + jnp.dot(items[1], items[3].T, preferred_element_type=jnp.float32)
        return (total + part.astype(jnp.bfloat16).astype(jnp.float32), None)
    input_grad, _ = lax.scan(in_step, jnp.zeros((TOKENS, D), jnp.float32), (gate_cb, linear_cb, gate_wb, linear_wb))
    x_blocks = inputs.reshape(N_DP, TOK_DEV, D)
    dy_blocks = out_cotangent.reshape(N_DP, TOK_DEV, D)
    g_blocks = gate_cot.reshape(N_DP, TOK_DEV, FF)
    l_blocks = linear_cot.reshape(N_DP, TOK_DEV, FF)
    h_blocks = hidden.reshape(N_DP, TOK_DEV, FF)

    def grad_step(totals, items):
        xb, dyb, gb, lb, hb = items
        one = jnp.dot(xb.T, gb, preferred_element_type=jnp.float32).astype(jnp.bfloat16).astype(jnp.float32)
        two = jnp.dot(xb.T, lb, preferred_element_type=jnp.float32).astype(jnp.bfloat16).astype(jnp.float32)
        three = jnp.dot(hb.T, dyb, preferred_element_type=jnp.float32).astype(jnp.bfloat16).astype(jnp.float32)
        return ((totals[0] + one, totals[1] + two, totals[2] + three), None)
    start = (jnp.zeros((D, FF), jnp.float32), jnp.zeros((D, FF), jnp.float32), jnp.zeros((FF, D), jnp.float32))
    grads, _ = lax.scan(grad_step, start, (x_blocks, dy_blocks, g_blocks, l_blocks, h_blocks))
    return (layer_output.astype(jnp.bfloat16), input_grad.astype(jnp.bfloat16), grads[0], grads[1], grads[2])
```

```python
import functools

import jax
import jax.numpy as jnp
from jax import lax
from jax.experimental import pallas as pl
from jax.experimental.pallas import tpu as pltpu
from jax.sharding import PartitionSpec as P

AXES = ("dp", "mp")
ZN, YN = 8, 4
BF = jnp.bfloat16
F32 = jnp.float32
VMEM_BYTES = 48 * 1024 * 1024


def position(device):
    dp, mp = divmod(device, 16)
    return dp // 8, dp % 8, mp // 8, (mp // 2) % 4, mp % 2


def number(x, z, y, core):
    x %= 4
    return ((x // 2) * 8 + z % 8) * 16 + (x % 2) * 8 + (y % 4) * 2 + core


def permutation(target):
    pairs = []
    for device in range(256):
        h, z, l, y, c = position(device)
        to = target(2 * h + l, h, z, l, y, c)
        if to is not None:
            pairs.append((device, number(*to)))
    return pairs


def inverse(pairs):
    return [(b, a) for a, b in pairs]


Z_UP = permutation(lambda x, h, z, l, y, c: (x, z + 1, y, c))
Z_DOWN = inverse(Z_UP)
Y_UP = permutation(lambda x, h, z, l, y, c: (x, z, y + 1, c))
Y_DOWN = inverse(Y_UP)
CORE = permutation(lambda x, h, z, l, y, c: (x, z, y, 1 - c))
WEIGHT = permutation(lambda x, h, z, l, y, c: (x + 1 if c == h else x - 1, z, y, h))
ACROSS = permutation(lambda x, h, z, l, y, c: (3 - x, z, y, c))
SPREAD = [
    permutation(lambda x, h, z, l, y, c: (x + 1, z, y, l) if c == l else (x, z, y, l)),
    permutation(lambda x, h, z, l, y, c: (x + 1, z, y, l) if c != l else None),
    permutation(lambda x, h, z, l, y, c: (x - 1, z, y, l) if c == l else None),
    permutation(lambda x, h, z, l, y, c: (x - 1, z, y, l) if c != l else None),
]
RELAY_UP = permutation(lambda x, h, z, l, y, c: (x + 1, z, y, c) if c != l else None)
RELAY_DOWN = permutation(lambda x, h, z, l, y, c: (x - 1, z, y, c) if c != l else None)


def move(value, pairs):
    return lax.ppermute(value, AXES, pairs)


def add(*terms):
    return functools.reduce(jnp.add, [t.astype(F32) for t in terms]).astype(BF)


ANY = pl.BlockSpec(memory_space=pl.ANY)
SMEM = pl.BlockSpec(memory_space=pltpu.SMEM)
VMEM = pl.BlockSpec(memory_space=pltpu.VMEM)
I_Z, I_Y, I_C, I_H, I_HA, I_L = range(6)


def run(copies, sems):
    started = []
    for i, (src, dst) in enumerate(copies):
        copy = pltpu.make_async_copy(src, dst, sems.at[i])
        copy.start()
        started.append(copy)
    for copy in started:
        copy.wait()


def block(j):
    return pl.ds(pl.multiple_of(j * 256, 256), 256)


def feature_copies(idx, pieces, xs):
    y, c, ha, l = idx[I_Y], idx[I_C], idx[I_HA], idx[I_L]
    copies = []
    for pair, step in zip(pieces, (0, 3, 1, 2)):
        row = lax.rem(y + step, YN)
        for which, (token, cores) in enumerate(((ha, (1 - l, l)), (1 - ha, (c, 1 - c)))):
            for slot in range(2):
                copies.append((pair[which].at[slot], xs.at[token, :, block(2 * row + cores[slot])]))
    return copies


def ring_copies(idx, pieces, places):
    z = idx[I_Z]
    return [(piece, places(lax.rem(z + ZN - s, ZN))) for s, piece in enumerate(pieces)]


def cot_copies(idx, local, pieces, ds):
    y, c, h = idx[I_Y], idx[I_C], idx[I_H]
    copies = [(local.at[:, pl.ds(pl.multiple_of(c * 2048, 2048), 2048)], ds.at[h])]
    for pair, step in zip(pieces, (0, 3, 1, 2)):
        row = lax.rem(y + step, YN)
        for half in range(2):
            copies.append((pair[half], ds.at[1 - h, :, block(2 * row + half)]))
    return copies


def pairs_of(refs):
    return [(refs[2 * i], refs[2 * i + 1]) for i in range(4)]


def dot(a, b, da=1, db=0):
    return lax.dot_general(a, b, (((da,), (db,)), ((), ())), preferred_element_type=F32)


def call(kernel, outs, scratch, n_sems, args, specs, flops, nbytes, name):
    return pl.pallas_call(
        kernel,
        out_shape=outs,
        in_specs=specs,
        out_specs=jax.tree.map(lambda _: VMEM, outs),
        scratch_shapes=[*scratch, pltpu.SemaphoreType.DMA((n_sems,))],
        compiler_params=pltpu.CompilerParams(vmem_limit_bytes=VMEM_BYTES),
        cost_estimate=pl.CostEstimate(flops=flops, bytes_accessed=nbytes, transcendentals=0),
        name=name,
    )(*args)


def shape(*dims, dtype=BF):
    return jax.ShapeDtypeStruct(dims, dtype)


def projection_kernel(*refs):
    idx, x, g, l = refs[0], refs[1:9], refs[9:17], refs[17:25]
    other, own, xs, gs, ls, sems = refs[25:]
    run(
        feature_copies(idx, pairs_of(x), xs)
        + ring_copies(idx, g, lambda j: gs.at[block(j), :])
        + ring_copies(idx, l, lambda j: ls.at[block(j), :]),
        sems,
    )
    c = idx[I_C]
    for out, token in ((other, 1 - c), (own, c)):
        out[:, :384] = dot(xs[token], gs[...])
        out[:, 384:] = dot(xs[token], ls[...])


def projections(idx, x, g, l):
    outs = [shape(384, 768, dtype=F32)] * 2
    scratch = [pltpu.VMEM((2, 384, 2048), BF), pltpu.VMEM((2048, 384), BF), pltpu.VMEM((2048, 384), BF)]
    return call(projection_kernel, outs, scratch, 32, (idx, *x, *g, *l), [SMEM] + [ANY] * 24, 2 * 768 * 2048 * 768, 9_000_000, "projections")


def hidden_cot_kernel(*refs):
    idx, local, pieces, o = refs[0], refs[1], refs[2:10], refs[10:18]
    other, own, ds, os, sems = refs[18:]
    run(cot_copies(idx, local, pairs_of(pieces), ds) + ring_copies(idx, o, lambda j: os.at[:, block(j)]), sems)
    c = idx[I_C]
    for out, token in ((other, 1 - c), (own, c)):
        out[...] = dot(ds[token], os[...], 1, 1)


def hidden_cots(idx, local, pieces, o):
    outs = [shape(384, 384, dtype=F32)] * 2
    scratch = [pltpu.VMEM((2, 384, 2048), BF), pltpu.VMEM((384, 2048), BF)]
    return call(hidden_cot_kernel, outs, scratch, 17, (idx, local, *pieces, *o), [SMEM] + [ANY] * 17, 2 * 768 * 2048 * 384, 6_000_000, "hidden_cots")


def own_and_other(idx, own, other, place):
    c = idx[I_C]
    return [(own, place(c)), (other, place(1 - c))]


def output_grad_kernel(*refs):
    idx, own, other, local, pieces = refs[0], refs[1], refs[2], refs[3], refs[4:12]
    out, hs, ds, sems = refs[12:]
    run(own_and_other(idx, own, other, hs.at.__getitem__) + cot_copies(idx, local, pairs_of(pieces), ds), sems)
    z = idx[I_Z]

    @pl.loop(0, ZN)
    def _(r):
        j = block(lax.rem(z + r, ZN))
        out[r] = (dot(hs[0], ds[0, :, j], 0, 0) + dot(hs[1], ds[1, :, j], 0, 0)).astype(BF)


def output_grads(idx, own, other, local, pieces):
    scratch = [pltpu.VMEM((2, 384, 384), BF), pltpu.VMEM((2, 384, 2048), BF)]
    return call(output_grad_kernel, shape(8, 384, 256), scratch, 11, (idx, own, other, local, *pieces), [SMEM] + [ANY] * 11, 2 * 768 * 2048 * 384, 6_000_000, "output_grads")


def input_weight_grad_kernel(*refs):
    idx, own, other, x = refs[0], refs[1], refs[2], refs[3:11]
    gate, linear, cs, xs, sems = refs[11:]
    run(own_and_other(idx, own, other, cs.at.__getitem__) + feature_copies(idx, pairs_of(x), xs), sems)
    z = idx[I_Z]

    @pl.loop(0, ZN)
    def _(r):
        j = block(lax.rem(z + r, ZN))
        both = dot(cs[0], xs[0, :, j], 0, 0) + dot(cs[1], xs[1, :, j], 0, 0)
        gate[r] = both[:384].astype(BF)
        linear[r] = both[384:].astype(BF)


def input_weight_grads(idx, own, other, x):
    scratch = [pltpu.VMEM((2, 384, 768), BF), pltpu.VMEM((2, 384, 2048), BF)]
    return call(input_weight_grad_kernel, [shape(8, 384, 256)] * 2, scratch, 18, (idx, own, other, *x), [SMEM] + [ANY] * 10, 2 * 768 * 2048 * 768, 8_000_000, "input_weight_grads")


def slot_of(idx, token, core):
    first = token == idx[I_HA]
    slot = jnp.where(first, (core == idx[I_L]).astype(jnp.int32), (core != idx[I_C]).astype(jnp.int32))
    return jnp.where(first, 0, 1), slot


def output_kernel(*refs):
    idx, own, other, o = refs[0], refs[1], refs[2], refs[3:11]
    out, hs, os, sems = refs[11:]
    run(own_and_other(idx, own, other, hs.at.__getitem__) + ring_copies(idx, o, lambda j: os.at[:, block(j)]), sems)
    y = idx[I_Y]

    @pl.loop(0, ZN)
    def _(j):
        step = lax.rem(j // 2 + YN - y, YN)
        for token in range(2):
            pair, slot = slot_of(idx, token, lax.rem(j, 2))
            out[step, pair, slot] = dot(hs[token], os[:, block(j)]).astype(BF)


def outputs(idx, own, other, o):
    scratch = [pltpu.VMEM((2, 384, 384), BF), pltpu.VMEM((384, 2048), BF)]
    return call(output_kernel, shape(4, 2, 2, 384, 256), scratch, 10, (idx, own, other, *o), [SMEM] + [ANY] * 10, 2 * 768 * 2048 * 384, 6_000_000, "outputs")


def input_grad_kernel(*refs):
    idx, own, other, g, l = refs[0], refs[1], refs[2], refs[3:11], refs[11:19]
    out, cs, gs, ls, sems = refs[19:]
    run(
        own_and_other(idx, own, other, cs.at.__getitem__)
        + ring_copies(idx, g, lambda j: gs.at[block(j), :])
        + ring_copies(idx, l, lambda j: ls.at[block(j), :]),
        sems,
    )
    y = idx[I_Y]

    @pl.loop(0, ZN)
    def _(j):
        step = lax.rem(j // 2 + YN - y, YN)
        for token in range(2):
            pair, slot = slot_of(idx, token, lax.rem(j, 2))
            value = dot(cs[token, :, :384], gs[block(j), :], 1, 1) + dot(cs[token, :, 384:], ls[block(j), :], 1, 1)
            out[2 * pair + slot, step] = value.astype(BF)


def input_grads(idx, own, other, g, l):
    scratch = [pltpu.VMEM((2, 384, 768), BF), pltpu.VMEM((2048, 384), BF), pltpu.VMEM((2048, 384), BF)]
    return call(input_grad_kernel, shape(4, 4, 384, 256), scratch, 18, (idx, own, other, *g, *l), [SMEM] + [ANY] * 18, 2 * 768 * 2048 * 768, 9_000_000, "input_grads")


def ring_gather(shard, up, down):
    held = [None] * ZN
    held[0] = shard
    for s in range(1, up + 1):
        held[s] = move(held[s - 1], Z_UP)
    value = shard
    for s in range(1, down + 1):
        value = move(value, Z_DOWN)
        held[ZN - s] = value
    return held


def ring_scatter(parts, up, down):
    value = parts[up]
    rising = move(value, Z_UP)
    for s in range(up - 1, 0, -1):
        rising = move(add(rising, parts[s]), Z_UP)
    falling = move(parts[ZN - down], Z_DOWN)
    for s in range(down - 1, 0, -1):
        falling = move(add(falling, parts[ZN - s]), Z_DOWN)
    return add(parts[0], rising, falling)


def gather_y(first, second):
    below = (move(first, Y_UP), move(second, Y_UP))
    above = (move(first, Y_DOWN), move(second, Y_DOWN))
    across = (move(below[0], Y_UP), move(above[1], Y_DOWN))
    return [first, second, *below, *above, *across]


def reduce_x(slots, is_l):
    up = move(slots[2], inverse(RELAY_UP))
    down = move(slots[3], inverse(RELAY_DOWN))
    sent = [add(slots[0], up), slots[1], slots[2], add(slots[3], down)]
    got = [move(s, inverse(pairs)) for s, pairs in zip(sent, SPREAD)]
    own = jnp.where(is_l, slots[1], jnp.zeros_like(slots[1]))
    return [own, *got]


def per_device(inputs, out_cotangent, gate_weight, linear_weight, output_weight):
    dp, mp = lax.axis_index("dp"), lax.axis_index("mp")
    h, z, l, y, c = dp // 8, dp % 8, mp // 8, (mp // 2) % 4, mp % 2
    is_l = c == l
    ha = jnp.where(is_l | (l == 1), h, 1 - h)
    idx = jnp.stack([z, y, c, h, ha, l]).astype(jnp.int32)

    g = ring_gather(move(gate_weight, WEIGHT), 4, 3)
    w = ring_gather(move(linear_weight, WEIGHT), 3, 4)
    o = ring_gather(move(output_weight, WEIGHT), 4, 3)

    got = [move(inputs, pairs) for pairs in SPREAD]
    relayed = (move(got[0], RELAY_UP), move(got[3], RELAY_DOWN))
    first = jnp.stack([got[0], jnp.where(is_l, inputs, got[1])])
    second = jnp.stack([jnp.where(is_l, relayed[0], got[2]), jnp.where(is_l, relayed[1], got[3])])
    x = gather_y(first, second)

    quarter = lax.dynamic_slice(out_cotangent, (0, c * 2048 + y * 512), (384, 512))
    cot = gather_y(move(quarter[:, :256], ACROSS), move(quarter[:, 256:], ACROSS))

    other, own = projections(idx, x, g, w)
    total = own + move(other, CORE)
    gate, linear = total[:, :384], total[:, 384:]
    k = 0.7978845608028654
    t = jnp.tanh(k * (gate + 0.044715 * gate * gate * gate))
    activated = 0.5 * gate * (1.0 + t)
    slope = 0.5 * (1.0 + t) + 0.5 * gate * (1.0 - t * t) * (k * (1.0 + 3 * 0.044715 * gate * gate))
    hidden = (activated * linear).astype(BF)
    slope = slope * linear
    hidden_far = move(hidden, CORE)
    og_parts = output_grads(idx, hidden, hidden_far, out_cotangent, cot)

    other, own = hidden_cots(idx, out_cotangent, cot, o)
    hidden_cot = own + move(other, CORE)
    cots = jnp.concatenate([hidden_cot * slope, hidden_cot * activated], axis=1).astype(BF)
    cots_far = move(cots, CORE)

    gate_parts, linear_parts = input_weight_grads(idx, cots, cots_far, x)
    out_parts = outputs(idx, hidden, hidden_far, o)
    in_parts = input_grads(idx, cots, cots_far, g, w)

    og = ring_scatter([og_parts[r] for r in range(ZN)], 4, 3)
    gg = ring_scatter([gate_parts[r] for r in range(ZN)], 4, 3)
    lg = ring_scatter([linear_parts[r] for r in range(ZN)], 3, 4)
    output_grad = move(og, inverse(WEIGHT)).astype(F32)
    gate_grad = move(gg, inverse(WEIGHT)).T.astype(F32)
    linear_grad = move(lg, inverse(WEIGHT)).T.astype(F32)

    far = (move(out_parts[2, 0], Y_UP), move(out_parts[2, 1], Y_DOWN))
    below = (move(add(out_parts[1, 0], far[0]), Y_UP), move(out_parts[1, 1], Y_UP))
    above = (move(out_parts[3, 0], Y_DOWN), move(add(out_parts[3, 1], far[1]), Y_DOWN))
    sums = [add(out_parts[0, i], below[i], above[i]) for i in range(2)]
    layer_output = add(*reduce_x([sums[0][0], sums[0][1], sums[1][0], sums[1][1]], is_l))

    terms = reduce_x([in_parts[s] for s in range(4)], is_l)
    rows = [add(*[t[r] for t in terms]) for r in range(YN)]
    below = move(add(rows[1], move(rows[2], Y_UP)), Y_UP)
    above = move(rows[3], Y_DOWN)
    input_grad = add(rows[0], below, above)
    return (layer_output, input_grad, gate_grad, linear_grad, output_grad)


def solution(mesh):
    return jax.shard_map(
        per_device,
        mesh=mesh,
        in_specs=(P("dp", "mp"), P("dp", None), P("dp", "mp"), P("dp", "mp"), P("mp", "dp")),
        out_specs=(P("dp", "mp"), P("dp", "mp"), P("dp", "mp"), P("dp", "mp"), P("mp", "dp")),
        check_vma=False,
    )
```

```python
import functools

import jax
import jax.numpy as jnp
from jax import lax
from jax.experimental import pallas as pl
from jax.experimental.pallas import tpu as pltpu
from jax.sharding import PartitionSpec as P

AXES = ("dp", "mp")
ZN, YN = 8, 4
BF = jnp.bfloat16
F32 = jnp.float32
VMEM_BYTES = 60 * 1024 * 1024


def position(device):
    dp, mp = divmod(device, 16)
    return dp // 8, dp % 8, mp // 8, (mp // 2) % 4, mp % 2


def number(x, z, y, core):
    x %= 4
    return ((x // 2) * 8 + z % 8) * 16 + (x % 2) * 8 + (y % 4) * 2 + core


def permutation(target):
    pairs = []
    for device in range(256):
        h, z, l, y, c = position(device)
        to = target(2 * h + l, h, z, l, y, c)
        if to is not None:
            pairs.append((device, number(*to)))
    return pairs


def inverse(pairs):
    return [(b, a) for a, b in pairs]


Z_UP = permutation(lambda x, h, z, l, y, c: (x, z + 1, y, c))
Z_DOWN = inverse(Z_UP)
CORE = permutation(lambda x, h, z, l, y, c: (x, z, y, 1 - c))
WEIGHT = permutation(lambda x, h, z, l, y, c: (x + 1 if c == h else x - 1, z, y, h))
ACROSS = permutation(lambda x, h, z, l, y, c: (3 - x, z, y, c))
FUSE = permutation(lambda x, h, z, l, y, c: (x, z, y, 1 - c) if c != l else None)
X_STEPS = [permutation(lambda x, h, z, l, y, c, d=d: (x + d, z, y, c) if c == l else None) for d in (1, -1, 2)]
Y_STEPS = [permutation(lambda x, h, z, l, y, c, d=d: (x, z, y + d, c)) for d in (1, -1, 2)]
Z_GROUPS = [list(range(8)), list(range(8, 16))]


def move(value, pairs):
    return lax.ppermute(value, AXES, pairs)


def add(*terms):
    return functools.reduce(jnp.add, [t.astype(F32) for t in terms]).astype(BF)


ANY = pl.BlockSpec(memory_space=pl.ANY)
SMEM = pl.BlockSpec(memory_space=pltpu.SMEM)
VMEM = pl.BlockSpec(memory_space=pltpu.VMEM)
I_Z, I_Y, I_C, I_H, I_HA, I_L = range(6)


def block(j):
    return pl.ds(pl.multiple_of(j * 256, 256), 256)


def rows_of(token):
    return pl.ds(pl.multiple_of(token * 384, 384), 384)


class Copies:
    def __init__(self, sems):
        self.sems, self.used = sems, 0

    def start(self, src, dst):
        copy = pltpu.make_async_copy(src, dst, self.sems.at[self.used])
        self.used += 1
        copy.start()
        return copy


def wait(copies):
    for copy in copies:
        copy.wait()


def dot(a, b, da=1, db=0):
    return lax.dot_general(a, b, (((da,), (db,)), ((), ())), preferred_element_type=F32)


def call(kernel, outs, scratch, n_sems, args, name, out_space=VMEM, near=()):
    return pl.pallas_call(
        kernel,
        out_shape=outs,
        in_specs=[SMEM] + [VMEM if i in near else ANY for i in range(1, len(args))],
        out_specs=jax.tree.map(lambda _: out_space, outs),
        scratch_shapes=[*scratch, pltpu.SemaphoreType.DMA((n_sems,))],
        compiler_params=pltpu.CompilerParams(vmem_limit_bytes=VMEM_BYTES),
        cost_estimate=pl.CostEstimate(flops=1000, bytes_accessed=1000, transcendentals=0),
        name=name,
    )(*args)


def shape(*dims, dtype=BF):
    return jax.ShapeDtypeStruct(dims, dtype)


STEPS = (0, 3, 1, 2)


def column(idx, step, slot):
    core = idx[I_C] if slot % 2 == 0 else 1 - idx[I_C]
    return 2 * lax.rem(idx[I_Y] + step, YN) + core


def token_of(idx, slot):
    return idx[I_HA] if slot < 2 else 1 - idx[I_HA]


def projection_kernel(idx, *refs):
    pieces, w = refs[:4], refs[4]
    far, own, xs, ws, sems = refs[5:]
    copies = Copies(sems)
    c = idx[I_C]
    features = []
    for place, token in enumerate((1 - c, c)):
        pair = jnp.where(token == idx[I_HA], 0, 2)
        for piece, step in zip(pieces, STEPS):
            for slot in range(2):
                features.append(copies.start(piece.at[pair + slot], xs.at[place, :, block(column(idx, step, slot))]))
        if place == 0:
            weights = [copies.start(w.at[:, pl.ds(256 * p, 256)], ws.at[p]) for p in range(3)]
    for place, out in enumerate((far, own)):
        wait(features[8 * place : 8 * place + 8])
        for p in range(3):
            if place == 0:
                weights[p].wait()
            out[:, 256 * p : 256 * p + 256] = dot(xs[place], ws[p].reshape(2048, 256))


def projections(idx, x, w):
    scratch = [pltpu.VMEM((2, 384, 2048), BF), pltpu.VMEM((3, 8, 256, 256), BF)]
    return call(projection_kernel, [shape(384, 768, dtype=F32)] * 2, scratch, 19, (idx, *x, w), "projections")


def output_weight_copies(copies, w, dst):
    return [copies.start(w.at[j, pl.ds(768, 384)], dst.at[:, 256 * j : 256 * j + 256]) for j in range(ZN)]


def cot_copies(copies, idx, local, remote, dst):
    c, h = idx[I_C], idx[I_H]
    half = pl.ds(pl.multiple_of(c * 2048, 2048), 2048)
    return [copies.start(local.at[:, half], dst.at[rows_of(h)]), copies.start(remote, dst.at[rows_of(1 - h)])]


def hidden_cot_kernel(idx, local, remote, w, other, own, ds, os, sems):
    copies = Copies(sems)
    wait(cot_copies(copies, idx, local, remote, ds) + output_weight_copies(copies, w, os))
    c = idx[I_C]
    other[...] = dot(ds[rows_of(1 - c)], os[...], 1, 1)
    own[...] = dot(ds[rows_of(c)], os[...], 1, 1)


def hidden_cots(idx, local, remote, w):
    outs = [shape(384, 384, dtype=F32)] * 2
    scratch = [pltpu.VMEM((768, 2048), BF), pltpu.VMEM((384, 2048), BF)]
    return call(hidden_cot_kernel, outs, scratch, 10, (idx, local, remote, w), "hidden_cots")


def activation_kernel(own, far, hidden, activated, slope):
    gate = own[:, :384] + far[:, :384]
    linear = own[:, 384:] + far[:, 384:]
    k = 0.7978845608028654
    t = jnp.tanh(k * (gate + 0.044715 * gate * gate * gate))
    half = 0.5 * (1.0 + t)
    value = gate * half
    activated[...] = value
    hidden[...] = (value * linear).astype(BF)
    slope[...] = linear * (half + 0.5 * gate * (1.0 - t * t) * (k * (1.0 + 3 * 0.044715 * gate * gate)))


def activation(own, far):
    return pl.pallas_call(
        activation_kernel,
        out_shape=[shape(384, 384), shape(384, 384, dtype=F32), shape(384, 384, dtype=F32)],
        cost_estimate=pl.CostEstimate(flops=1000, bytes_accessed=1000, transcendentals=0),
        name="activation",
    )(own, far)


def cot_kernel(own, far, activated, slope, cots):
    cot = own[...] + far[...]
    cots[:, :384] = (cot * slope[...]).astype(BF)
    cots[:, 384:] = (cot * activated[...]).astype(BF)


def cotangents(own, far, activated, slope):
    return pl.pallas_call(
        cot_kernel,
        out_shape=shape(384, 768),
        cost_estimate=pl.CostEstimate(flops=1000, bytes_accessed=1000, transcendentals=0),
        name="cotangents",
    )(own, far, activated, slope)


def stack_tokens(idx, own, other, dst):
    dst[rows_of(idx[I_C])] = own[...]
    dst[rows_of(1 - idx[I_C])] = other[...]


def transposed(idx, own, other, dst):
    dst[:, rows_of(idx[I_C])] = own[...].T
    dst[:, rows_of(1 - idx[I_C])] = other[...].T


def weight_grad_kernel(idx, hidden, hidden_far, cots, cots_far, local, remote, *refs):
    pieces = refs[:4]
    out, ht, ct, ds, xs, stage, sems = refs[4:]
    copies = Copies(sems)
    out_cots = cot_copies(copies, idx, local, remote, ds)
    arriving = []
    for piece, step in zip(pieces, STEPS):
        for core in range(2):
            j = column(idx, step, core)
            both = [copies.start(piece.at[slot], xs.at[rows_of(token_of(idx, slot)), block(j)]) for slot in (core, 2 + core)]
            arriving.append((j, both))
    transposed(idx, hidden, hidden_far, ht)
    transposed(idx, cots, cots_far, ct)
    wait(out_cots)
    for j in range(ZN):
        stage[j, 768:] = dot(ht[...], ds[:, 256 * j : 256 * j + 256]).astype(BF)
    leaving = []
    for j, both in arriving:
        wait(both)
        stage[j, :768] = dot(ct[...], xs[:, block(j)]).astype(BF)
        leaving.append(copies.start(stage.at[j], out.at[j]))
    wait(leaving)


def weight_grads(idx, hidden, hidden_far, cots, cots_far, local, remote, x):
    half = pltpu.VMEM((768, 2048), BF)
    scratch = [pltpu.VMEM((384, 768), BF), pltpu.VMEM((768, 768), BF), half, half, pltpu.VMEM((8, 1152, 256), BF)]
    args = (idx, hidden, hidden_far, cots, cots_far, local, remote, *x)
    return call(weight_grad_kernel, shape(8, 1152, 256), scratch, 26, args, "weight_grads", ANY, (1, 2, 3, 4))


def output_kernel(idx, own, other, w, here, up, down, across_up, across_down, hs, os, sems):
    copies = Copies(sems)
    weights = output_weight_copies(copies, w, os)
    stack_tokens(idx, own, other, hs)
    wait(weights)
    for step, out in ((0, here), (1, up), (3, down), (2, None)):
        for slot in range(4):
            value = dot(hs[rows_of(token_of(idx, slot))], os[:, block(column(idx, step, slot))]).astype(BF)
            if out is not None:
                out[slot] = value
            else:
                (across_up, across_down)[slot // 2][slot % 2] = value


def outputs(idx, own, other, w):
    outs = [shape(4, 384, 256)] * 3 + [shape(2, 384, 256)] * 2
    scratch = [pltpu.VMEM((768, 384), BF), pltpu.VMEM((384, 2048), BF)]
    return call(output_kernel, outs, scratch, 8, (idx, own, other, w), "outputs", near=(1, 2))


def input_grad_kernel(idx, own, other, w, first, second, cs, ws, sf, ss, sems):
    copies = Copies(sems)
    weights = [copies.start(w.at[:, pl.ds(256 * p, 256)], ws.at[:, :, 256 * p : 256 * p + 256]) for p in range(3)]
    stack_tokens(idx, own, other, cs)
    wait(weights)
    leaving = []
    for step in range(YN):
        for core in range(2):
            j = column(idx, step, core)
            for pair, (stage, out) in enumerate(((sf, first), (ss, second))):
                stage[core, step] = dot(cs[rows_of(token_of(idx, 2 * pair))], ws[j], 1, 1).astype(BF)
                leaving.append(copies.start(stage.at[core, step], out.at[core, step]))
    wait(leaving)


def input_grads(idx, own, other, w):
    stage = pltpu.VMEM((2, 4, 384, 256), BF)
    scratch = [pltpu.VMEM((768, 768), BF), pltpu.VMEM((8, 256, 768), BF), stage, stage]
    return call(input_grad_kernel, [shape(2, 4, 384, 256)] * 2, scratch, 19, (idx, own, other, w), "input_grads", ANY, (1, 2))


def pack_kernel(gate, linear, out, packed):
    packed[0:256] = gate[:, 0:256]
    packed[256:512, 0:128] = gate[:, 256:384]
    packed[256:512, 128:256] = linear[:, 0:128]
    packed[512:768] = linear[:, 128:384]
    packed[768:1152] = out[...]


def pack(gate, linear, out):
    return pl.pallas_call(pack_kernel, out_shape=shape(1152, 256), name="pack")(gate, linear, out)


def finish_kernel(share, gate, linear, out):
    gate[...] = share[:384].astype(F32).T
    linear[...] = share[384:768].astype(F32).T
    out[...] = share[768:].astype(F32)


def finish(share):
    outs = [shape(256, 384, dtype=F32), shape(256, 384, dtype=F32), shape(384, 256, dtype=F32)]
    cost = pl.CostEstimate(flops=0, bytes_accessed=50_000_000, transcendentals=0)
    return pl.pallas_call(finish_kernel, out_shape=outs, cost_estimate=cost, name="finish")(share)


def sum_x(first, second):
    from_above = move(first, inverse(X_STEPS[0]))
    from_below = move(second, inverse(X_STEPS[1]))
    from_across = move(second, X_STEPS[2])
    return add(first, from_above, from_below, from_across)


def split(total, is_l):
    return jnp.where(is_l, total[0], move(total[1], inverse(FUSE)))


def per_device(inputs, out_cotangent, gate_weight, linear_weight, output_weight):
    dp, mp = lax.axis_index("dp"), lax.axis_index("mp")
    h, z, l, y, c = dp // 8, dp % 8, mp // 8, (mp // 2) % 4, mp % 2
    is_l = c == l
    ha = jnp.where(is_l | (l == 1), h, 1 - h)
    idx = jnp.stack([z, y, c, h, ha, l]).astype(jnp.int32)

    shard = move(pack(gate_weight, linear_weight, output_weight), WEIGHT)
    mine = jnp.stack([inputs, move(inputs, FUSE)])
    shard, mine = lax.optimization_barrier((shard, mine))
    w = lax.all_gather(shard, "dp", axis_index_groups=Z_GROUPS)
    below, above, across = [move(mine, pairs) for pairs in X_STEPS]
    half = lax.dynamic_slice(out_cotangent, (0, c * 2048), (384, 2048))
    slots = jnp.concatenate([jnp.where(is_l, mine, below), jnp.where(is_l, across, above)])
    slots, half = lax.optimization_barrier((slots, half))
    x = [slots, *[move(slots, pairs) for pairs in Y_STEPS]]
    remote = move(half, ACROSS)

    far, own = projections(idx, x, w)
    idx, far = lax.optimization_barrier((idx, far))
    far = move(far, CORE)
    hc_far, hc_own = hidden_cots(idx, out_cotangent, remote, w)
    hc_far = move(hc_far, CORE)
    hidden, activated, slope = activation(own, far)
    hidden_far = move(hidden, CORE)
    hc_far, activated = lax.optimization_barrier((hc_far, activated))
    cots = cotangents(hc_own, hc_far, activated, slope)
    cots_far = move(cots, CORE)

    hidden_far, cots = lax.optimization_barrier((hidden_far, cots))
    here, up, down, across_up, across_down = outputs(idx, hidden, hidden_far, w)
    idx, across_up, across_down = lax.optimization_barrier((idx, across_up, across_down))
    parts = weight_grads(idx, hidden, hidden_far, cots, cots_far, out_cotangent, remote, x)
    idx, parts = lax.optimization_barrier((idx, parts))
    share = lax.psum_scatter(parts.reshape(8 * 1152, 256), "dp", scatter_dimension=0, axis_index_groups=Z_GROUPS, tiled=True)
    first, second = input_grads(idx, cots, cots_far, w)

    zero = jnp.zeros((), BF)
    up = add(up, lax.pad(move(across_up, Y_STEPS[0]), zero, ((0, 2, 0), (0, 0, 0), (0, 0, 0))))
    down = add(down, lax.pad(move(across_down, Y_STEPS[1]), zero, ((2, 0, 0), (0, 0, 0), (0, 0, 0))))
    sums = add(here, move(up, Y_STEPS[0]), move(down, Y_STEPS[1]))

    layer_output = split(sum_x(sums[:2], sums[2:]), is_l)

    total = sum_x(first, second)
    total, share = lax.optimization_barrier((total, share))
    gate_grad, linear_grad, output_grad = finish(move(share, inverse(WEIGHT)))
    rows = split(total, is_l)
    input_grad = add(rows[0], move(rows[1], Y_STEPS[0]), move(rows[3], Y_STEPS[1]), move(rows[2], Y_STEPS[2]))
    return (layer_output, input_grad, gate_grad, linear_grad, output_grad)


def solution(mesh):
    return jax.shard_map(
        per_device,
        mesh=mesh,
        in_specs=(P("dp", "mp"), P("dp", None), P("dp", "mp"), P("dp", "mp"), P("mp", "dp")),
        out_specs=(P("dp", "mp"), P("dp", "mp"), P("dp", "mp"), P("dp", "mp"), P("mp", "dp")),
        check_vma=False,
    )
```

```python
import functools

import jax
import jax.numpy as jnp
from jax import lax
from jax.experimental import pallas as pl
from jax.experimental.pallas import tpu as pltpu
from jax.sharding import PartitionSpec as P

AXES = ("dp", "mp")
ZN, YN = 8, 4
BF = jnp.bfloat16
F32 = jnp.float32
VMEM_BYTES = 63 * 1024 * 1024


def position(device):
    dp, mp = divmod(device, 16)
    return dp // 8, dp % 8, mp // 8, (mp // 2) % 4, mp % 2


def number(x, z, y, core):
    x %= 4
    return ((x // 2) * 8 + z % 8) * 16 + (x % 2) * 8 + (y % 4) * 2 + core


def permutation(target):
    pairs = []
    for device in range(256):
        h, z, l, y, c = position(device)
        to = target(2 * h + l, h, z, l, y, c)
        if to is not None:
            pairs.append((device, number(*to)))
    return pairs


def inverse(pairs):
    return [(b, a) for a, b in pairs]


Z_UP = permutation(lambda x, h, z, l, y, c: (x, z + 1, y, c))
Z_DOWN = inverse(Z_UP)
CORE = permutation(lambda x, h, z, l, y, c: (x, z, y, 1 - c))
WEIGHT = permutation(lambda x, h, z, l, y, c: (x + 1 if c == h else x - 1, z, y, h))
ACROSS = permutation(lambda x, h, z, l, y, c: (3 - x, z, y, c))
FUSE = permutation(lambda x, h, z, l, y, c: (x, z, y, 1 - c) if c != l else None)
X_STEPS = [permutation(lambda x, h, z, l, y, c, d=d: (x + d, z, y, c) if c == l else None) for d in (1, -1, 2)]
Y_STEPS = [permutation(lambda x, h, z, l, y, c, d=d: (x, z, y + d, c)) for d in (1, -1, 2)]
Z_GROUPS = [list(range(8)), list(range(8, 16))]


def move(value, pairs):
    return lax.ppermute(value, AXES, pairs)


def add(*terms):
    return functools.reduce(jnp.add, [t.astype(F32) for t in terms]).astype(BF)


ANY = pl.BlockSpec(memory_space=pl.ANY)
SMEM = pl.BlockSpec(memory_space=pltpu.SMEM)
VMEM = pl.BlockSpec(memory_space=pltpu.VMEM)
I_Z, I_Y, I_C, I_H, I_HA, I_L = range(6)


def block(j):
    return pl.ds(pl.multiple_of(j * 256, 256), 256)


def rows_of(token):
    return pl.ds(pl.multiple_of(token * 384, 384), 384)


class Copies:
    def __init__(self, sems):
        self.sems, self.used = sems, 0

    def start(self, src, dst):
        copy = pltpu.make_async_copy(src, dst, self.sems.at[self.used])
        self.used += 1
        copy.start()
        return copy


def wait(copies):
    for copy in copies:
        copy.wait()


def dot(a, b, da=1, db=0):
    return lax.dot_general(a, b, (((da,), (db,)), ((), ())), preferred_element_type=F32)


def call(kernel, outs, scratch, n_sems, args, name, out_space=VMEM, near=(), traffic=1000):
    return pl.pallas_call(
        kernel,
        out_shape=outs,
        in_specs=[SMEM] + [VMEM if i in near else ANY for i in range(1, len(args))],
        out_specs=jax.tree.map(lambda _: out_space, outs),
        scratch_shapes=[*scratch, pltpu.SemaphoreType.DMA((n_sems,))],
        compiler_params=pltpu.CompilerParams(vmem_limit_bytes=VMEM_BYTES),
        cost_estimate=pl.CostEstimate(flops=1000, bytes_accessed=traffic, transcendentals=0),
        name=name,
    )(*args)


def shape(*dims, dtype=BF):
    return jax.ShapeDtypeStruct(dims, dtype)


STEPS = (0, 3, 1, 2)


def column(idx, step, slot):
    core = idx[I_C] if slot % 2 == 0 else 1 - idx[I_C]
    return 2 * lax.rem(idx[I_Y] + step, YN) + core


def token_of(idx, slot):
    return idx[I_HA] if slot < 2 else 1 - idx[I_HA]


def projection_kernel(idx, *refs):
    pieces, w = refs[:4], refs[4]
    far, own, xs, ws, sems = refs[5:]
    copies = Copies(sems)
    c = idx[I_C]
    features = []
    for place, token in enumerate((1 - c, c)):
        pair = jnp.where(token == idx[I_HA], 0, 2)
        for piece, step in zip(pieces, STEPS):
            for slot in range(2):
                features.append(copies.start(piece.at[pair + slot], xs.at[place, :, block(column(idx, step, slot))]))
        if place == 0:
            weights = [copies.start(w.at[:, pl.ds(256 * p, 256)], ws.at[p]) for p in range(3)]
    for place, out in enumerate((far, own)):
        wait(features[8 * place : 8 * place + 8])
        for p in range(3):
            if place == 0:
                weights[p].wait()
            out[:, 256 * p : 256 * p + 256] = dot(xs[place], ws[p].reshape(2048, 256))


def projections(idx, x, w):
    scratch = [pltpu.VMEM((2, 384, 2048), BF), pltpu.VMEM((3, 8, 256, 256), BF)]
    return call(projection_kernel, [shape(384, 768, dtype=F32)] * 2, scratch, 19, (idx, *x, w), "projections")


def output_weight_copies(copies, w, dst):
    return [copies.start(w.at[j, pl.ds(768, 384)], dst.at[:, 256 * j : 256 * j + 256]) for j in range(ZN)]


def cot_copies(copies, idx, local, remote, dst):
    c, h = idx[I_C], idx[I_H]
    half = pl.ds(pl.multiple_of(c * 2048, 2048), 2048)
    return [copies.start(local.at[:, half], dst.at[rows_of(h)]), copies.start(remote, dst.at[rows_of(1 - h)])]


def hidden_cot_kernel(idx, local, remote, w, other, own, ds, os, sems):
    copies = Copies(sems)
    wait(cot_copies(copies, idx, local, remote, ds) + output_weight_copies(copies, w, os))
    c = idx[I_C]
    other[...] = dot(ds[rows_of(1 - c)], os[...], 1, 1)
    own[...] = dot(ds[rows_of(c)], os[...], 1, 1)


def hidden_cots(idx, local, remote, w):
    outs = [shape(384, 384, dtype=F32)] * 2
    scratch = [pltpu.VMEM((768, 2048), BF), pltpu.VMEM((384, 2048), BF)]
    return call(hidden_cot_kernel, outs, scratch, 10, (idx, local, remote, w), "hidden_cots")


def activation_kernel(own, far, hc_own, hc_far, hidden, cots):
    gate = own[:, :384] + far[:, :384]
    linear = own[:, 384:] + far[:, 384:]
    k = 0.7978845608028654
    t = jnp.tanh(k * (gate + 0.044715 * gate * gate * gate))
    half = 0.5 * (1.0 + t)
    activated = gate * half
    slope = half + 0.5 * gate * (1.0 - t * t) * (k * (1.0 + 3 * 0.044715 * gate * gate))
    hidden[...] = (activated * linear).astype(BF)
    cot = hc_own[...] + hc_far[...]
    cots[:, :384] = (cot * linear * slope).astype(BF)
    cots[:, 384:] = (cot * activated).astype(BF)


def activation(own, far, hc_own, hc_far):
    return pl.pallas_call(
        activation_kernel,
        out_shape=[shape(384, 384), shape(384, 768)],
        cost_estimate=pl.CostEstimate(flops=1000, bytes_accessed=1000, transcendentals=0),
        name="activation",
    )(own, far, hc_own, hc_far)


def stack_tokens(idx, own, other, dst):
    dst[rows_of(idx[I_C])] = own[...]
    dst[rows_of(1 - idx[I_C])] = other[...]


def transposed(idx, own, other, dst):
    dst[:, rows_of(idx[I_C])] = own[...].T
    dst[:, rows_of(1 - idx[I_C])] = other[...].T


def weight_grad_kernel(idx, hidden, hidden_far, cots, cots_far, local, remote, *refs):
    pieces = refs[:4]
    out, ht, ct, ds, xs, stage, sems = refs[4:]
    copies = Copies(sems)
    loads = cot_copies(copies, idx, local, remote, ds)
    for piece, step in zip(pieces, STEPS):
        for slot in range(4):
            dst = xs.at[rows_of(token_of(idx, slot)), block(column(idx, step, slot))]
            loads.append(copies.start(piece.at[slot], dst))
    transposed(idx, hidden, hidden_far, ht)
    transposed(idx, cots, cots_far, ct)
    wait(loads)
    leaving = []
    for j in range(ZN):
        columns = slice(256 * j, 256 * j + 256)
        stage[j, :768] = dot(ct[...], xs[:, columns]).astype(BF)
        stage[j, 768:] = dot(ht[...], ds[:, columns]).astype(BF)
        leaving.append(copies.start(stage.at[j], out.at[j]))
    wait(leaving)


def weight_grads(idx, hidden, hidden_far, cots, cots_far, local, remote, x):
    half = pltpu.VMEM((768, 2048), BF)
    scratch = [pltpu.VMEM((384, 768), BF), pltpu.VMEM((768, 768), BF), half, half, pltpu.VMEM((8, 1152, 256), BF)]
    args = (idx, hidden, hidden_far, cots, cots_far, local, remote, *x)
    return call(weight_grad_kernel, shape(8, 1152, 256), scratch, 26, args, "weight_grads", ANY, (1, 2, 3, 4))


def output_kernel(idx, own, other, w, here, up, down, across_up, across_down, hs, os, sems):
    copies = Copies(sems)
    weights = output_weight_copies(copies, w, os)
    stack_tokens(idx, own, other, hs)
    wait(weights)
    for step, out in ((0, here), (1, up), (3, down), (2, None)):
        for slot in range(4):
            value = dot(hs[rows_of(token_of(idx, slot))], os[:, block(column(idx, step, slot))]).astype(BF)
            if out is not None:
                out[slot] = value
            else:
                (across_up, across_down)[slot // 2][slot % 2] = value


def outputs(idx, own, other, w):
    outs = [shape(4, 384, 256)] * 3 + [shape(2, 384, 256)] * 2
    scratch = [pltpu.VMEM((768, 384), BF), pltpu.VMEM((384, 2048), BF)]
    return call(output_kernel, outs, scratch, 8, (idx, own, other, w), "outputs", near=(1, 2), traffic=40_000_000)


def input_grad_kernel(idx, own, other, w, first, second, cs, ws, sf, ss, sems):
    copies = Copies(sems)
    weights = [copies.start(w.at[:, pl.ds(256 * p, 256)], ws.at[:, :, 256 * p : 256 * p + 256]) for p in range(3)]
    stack_tokens(idx, own, other, cs)
    wait(weights)
    leaving = []
    for step in range(YN):
        for core in range(2):
            j = column(idx, step, core)
            for pair, (stage, out) in enumerate(((sf, first), (ss, second))):
                stage[core, step] = dot(cs[rows_of(token_of(idx, 2 * pair))], ws[j], 1, 1).astype(BF)
                leaving.append(copies.start(stage.at[core, step], out.at[core, step]))
    wait(leaving)


def input_grads(idx, own, other, w):
    stage = pltpu.VMEM((2, 4, 384, 256), BF)
    scratch = [pltpu.VMEM((768, 768), BF), pltpu.VMEM((8, 256, 768), BF), stage, stage]
    return call(input_grad_kernel, [shape(2, 4, 384, 256)] * 2, scratch, 19, (idx, own, other, w), "input_grads", ANY, (1, 2))


def pack_kernel(gate, linear, out, packed):
    packed[0:256] = gate[:, 0:256]
    packed[256:512, 0:128] = gate[:, 256:384]
    packed[256:512, 128:256] = linear[:, 0:128]
    packed[512:768] = linear[:, 128:384]
    packed[768:1152] = out[...]


def pack(gate, linear, out):
    return pl.pallas_call(pack_kernel, out_shape=shape(1152, 256), name="pack")(gate, linear, out)


def finish_kernel(share, gate, linear, out):
    gate[...] = share[:384].astype(F32).T
    linear[...] = share[384:768].astype(F32).T
    out[...] = share[768:].astype(F32)


def finish(share):
    outs = [shape(256, 384, dtype=F32), shape(256, 384, dtype=F32), shape(384, 256, dtype=F32)]
    cost = pl.CostEstimate(flops=0, bytes_accessed=50_000_000, transcendentals=0)
    return pl.pallas_call(finish_kernel, out_shape=outs, cost_estimate=cost, name="finish")(share)


def sum_x(first, second):
    from_above = move(first, inverse(X_STEPS[0]))
    from_below = move(second, inverse(X_STEPS[1]))
    from_across = move(second, X_STEPS[2])
    return add(first, from_above, from_below, from_across)


def split(total, is_l):
    return jnp.where(is_l, total[0], move(total[1], inverse(FUSE)))


def per_device(inputs, out_cotangent, gate_weight, linear_weight, output_weight):
    dp, mp = lax.axis_index("dp"), lax.axis_index("mp")
    h, z, l, y, c = dp // 8, dp % 8, mp // 8, (mp // 2) % 4, mp % 2
    is_l = c == l
    ha = jnp.where(is_l | (l == 1), h, 1 - h)
    idx = jnp.stack([z, y, c, h, ha, l]).astype(jnp.int32)

    shard = move(pack(gate_weight, linear_weight, output_weight), WEIGHT)
    mine = jnp.stack([inputs, move(inputs, FUSE)])
    shard, mine = lax.optimization_barrier((shard, mine))
    w = lax.all_gather(shard, "dp", axis_index_groups=Z_GROUPS)
    below, above, across = [move(mine, pairs) for pairs in X_STEPS]
    half = lax.dynamic_slice(out_cotangent, (0, c * 2048), (384, 2048))
    slots = jnp.concatenate([jnp.where(is_l, mine, below), jnp.where(is_l, across, above)])
    slots, half = lax.optimization_barrier((slots, half))
    x = [slots, *[move(slots, pairs) for pairs in Y_STEPS]]
    remote = move(half, ACROSS)

    far, own = projections(idx, x, w)
    idx, far = lax.optimization_barrier((idx, far))
    far = move(far, CORE)
    hc_far, hc_own = hidden_cots(idx, out_cotangent, remote, w)
    hc_far = move(hc_far, CORE)
    hidden, cots = activation(own, far, hc_own, hc_far)
    hidden_far = move(hidden, CORE)
    cots_far = move(cots, CORE)

    parts = weight_grads(idx, hidden, hidden_far, cots, cots_far, out_cotangent, remote, x)
    idx, parts = lax.optimization_barrier((idx, parts))
    share = lax.psum_scatter(parts.reshape(8 * 1152, 256), "dp", scatter_dimension=0, axis_index_groups=Z_GROUPS, tiled=True)
    first, second = input_grads(idx, cots, cots_far, w)
    idx, first, second = lax.optimization_barrier((idx, first, second))
    here, up, down, across_up, across_down = outputs(idx, hidden, hidden_far, w)

    zero = jnp.zeros((), BF)
    up = add(up, lax.pad(move(across_up, Y_STEPS[0]), zero, ((0, 2, 0), (0, 0, 0), (0, 0, 0))))
    down = add(down, lax.pad(move(across_down, Y_STEPS[1]), zero, ((2, 0, 0), (0, 0, 0), (0, 0, 0))))
    sums = add(here, move(up, Y_STEPS[0]), move(down, Y_STEPS[1]))

    layer_output = split(sum_x(sums[:2], sums[2:]), is_l)

    total = sum_x(first, second)
    total, share = lax.optimization_barrier((total, share))
    gate_grad, linear_grad, output_grad = finish(move(share, inverse(WEIGHT)))
    rows = split(total, is_l)
    input_grad = add(rows[0], move(rows[1], Y_STEPS[0]), move(rows[3], Y_STEPS[1]), move(rows[2], Y_STEPS[2]))
    return (layer_output, input_grad, gate_grad, linear_grad, output_grad)


def solution(mesh):
    return jax.shard_map(
        per_device,
        mesh=mesh,
        in_specs=(P("dp", "mp"), P("dp", None), P("dp", "mp"), P("dp", "mp"), P("mp", "dp")),
        out_specs=(P("dp", "mp"), P("dp", "mp"), P("dp", "mp"), P("dp", "mp"), P("mp", "dp")),
        check_vma=False,
    )
```

```python
import functools

import jax
import jax.numpy as jnp
from jax import lax
from jax.experimental import pallas as pl
from jax.experimental.pallas import tpu as pltpu
from jax.sharding import PartitionSpec as P

AXES = ("dp", "mp")
ZN, YN = 8, 4
BF = jnp.bfloat16
F32 = jnp.float32
VMEM_BYTES = 63 * 1024 * 1024


def position(device):
    dp, mp = divmod(device, 16)
    return dp // 8, dp % 8, mp // 8, (mp // 2) % 4, mp % 2


def number(x, z, y, core):
    x %= 4
    return ((x // 2) * 8 + z % 8) * 16 + (x % 2) * 8 + (y % 4) * 2 + core


def permutation(target):
    pairs = []
    for device in range(256):
        h, z, l, y, c = position(device)
        to = target(2 * h + l, h, z, l, y, c)
        if to is not None:
            pairs.append((device, number(*to)))
    return pairs


def inverse(pairs):
    return [(b, a) for a, b in pairs]


Z_UP = permutation(lambda x, h, z, l, y, c: (x, z + 1, y, c))
Z_DOWN = inverse(Z_UP)
CORE = permutation(lambda x, h, z, l, y, c: (x, z, y, 1 - c))
WEIGHT = permutation(lambda x, h, z, l, y, c: (x + 1 if c == h else x - 1, z, y, h))
ACROSS = permutation(lambda x, h, z, l, y, c: (3 - x, z, y, c))
FUSE = permutation(lambda x, h, z, l, y, c: (x, z, y, 1 - c) if c != l else None)
X_STEPS = [permutation(lambda x, h, z, l, y, c, d=d: (x + d, z, y, c) if c == l else None) for d in (1, -1, 2)]
Y_STEPS = [permutation(lambda x, h, z, l, y, c, d=d: (x, z, y + d, c)) for d in (1, -1, 2)]
Z_GROUPS = [list(range(8)), list(range(8, 16))]


def move(value, pairs):
    return lax.ppermute(value, AXES, pairs)


def add(*terms):
    return functools.reduce(jnp.add, [t.astype(F32) for t in terms]).astype(BF)


ANY = pl.BlockSpec(memory_space=pl.ANY)
SMEM = pl.BlockSpec(memory_space=pltpu.SMEM)
VMEM = pl.BlockSpec(memory_space=pltpu.VMEM)
I_Z, I_Y, I_C, I_H, I_HA, I_L = range(6)


def block(j):
    return pl.ds(pl.multiple_of(j * 256, 256), 256)


def rows_of(token):
    return pl.ds(pl.multiple_of(token * 384, 384), 384)


class Copies:
    def __init__(self, sems):
        self.sems, self.used = sems, 0

    def start(self, src, dst):
        copy = pltpu.make_async_copy(src, dst, self.sems.at[self.used])
        self.used += 1
        copy.start()
        return copy


def wait(copies):
    for copy in copies:
        copy.wait()


def dot(a, b, da=1, db=0):
    return lax.dot_general(a, b, (((da,), (db,)), ((), ())), preferred_element_type=F32)


def call(kernel, outs, scratch, n_sems, args, name, out_space=VMEM, near=(), traffic=1000):
    return pl.pallas_call(
        kernel,
        out_shape=outs,
        in_specs=[SMEM] + [VMEM if i in near else ANY for i in range(1, len(args))],
        out_specs=jax.tree.map(lambda _: out_space, outs),
        scratch_shapes=[*scratch, pltpu.SemaphoreType.DMA((n_sems,))],
        compiler_params=pltpu.CompilerParams(vmem_limit_bytes=VMEM_BYTES),
        cost_estimate=pl.CostEstimate(flops=1000, bytes_accessed=traffic, transcendentals=0),
        name=name,
    )(*args)


def shape(*dims, dtype=BF):
    return jax.ShapeDtypeStruct(dims, dtype)


STEPS = (0, 3, 1, 2)


def column(idx, step, slot):
    core = idx[I_C] if slot % 2 == 0 else 1 - idx[I_C]
    return 2 * lax.rem(idx[I_Y] + step, YN) + core


def token_of(idx, slot):
    return idx[I_HA] if slot < 2 else 1 - idx[I_HA]


def projection_kernel(idx, *refs):
    pieces, w = refs[:4], refs[4]
    far, own, xs, ws, stage, sems = refs[5:]
    copies = Copies(sems)
    c = idx[I_C]
    features = []
    for place, token in enumerate((1 - c, c)):
        pair = jnp.where(token == idx[I_HA], 0, 2)
        for piece, step in zip(pieces, STEPS):
            for slot in range(2):
                features.append(copies.start(piece.at[pair + slot], xs.at[place, :, block(column(idx, step, slot))]))
        if place == 0:
            weights = [copies.start(w.at[:, pl.ds(256 * p, 256)], ws.at[p]) for p in range(3)]
    leaving = []
    for place, out in enumerate((far, own)):
        wait(features[8 * place : 8 * place + 8])
        for p in range(3):
            if place == 0:
                weights[p].wait()
            stage[place, :, 256 * p : 256 * p + 256] = dot(xs[place], ws[p].reshape(2048, 256))
        leaving.append(copies.start(stage.at[place], out))
    wait(leaving)


def projections(idx, x, w):
    scratch = [pltpu.VMEM((2, 384, 2048), BF), pltpu.VMEM((3, 8, 256, 256), BF), pltpu.VMEM((2, 384, 768), F32)]
    return call(projection_kernel, [shape(384, 768, dtype=F32)] * 2, scratch, 21, (idx, *x, w), "projections", ANY)


def output_weight_copies(copies, w, dst):
    return [copies.start(w.at[j, pl.ds(768, 384)], dst.at[:, 256 * j : 256 * j + 256]) for j in range(ZN)]


def cot_copies(copies, idx, local, remote, dst):
    c, h = idx[I_C], idx[I_H]
    half = pl.ds(pl.multiple_of(c * 2048, 2048), 2048)
    return [copies.start(local.at[:, half], dst.at[rows_of(h)]), copies.start(remote, dst.at[rows_of(1 - h)])]


def hidden_cot_kernel(idx, local, remote, w, other, own, ds, os, sems):
    copies = Copies(sems)
    wait(cot_copies(copies, idx, local, remote, ds) + output_weight_copies(copies, w, os))
    c = idx[I_C]
    other[...] = dot(ds[rows_of(1 - c)], os[...], 1, 1)
    own[...] = dot(ds[rows_of(c)], os[...], 1, 1)


def hidden_cots(idx, local, remote, w):
    outs = [shape(384, 384, dtype=F32)] * 2
    scratch = [pltpu.VMEM((768, 2048), BF), pltpu.VMEM((384, 2048), BF)]
    return call(hidden_cot_kernel, outs, scratch, 10, (idx, local, remote, w), "hidden_cots")


def activation_kernel(own, far, hc_own, hc_far, hidden, cots):
    gate = own[:, :384] + far[:, :384]
    linear = own[:, 384:] + far[:, 384:]
    k = 0.7978845608028654
    t = jnp.tanh(k * (gate + 0.044715 * gate * gate * gate))
    half = 0.5 * (1.0 + t)
    activated = gate * half
    slope = half + 0.5 * gate * (1.0 - t * t) * (k * (1.0 + 3 * 0.044715 * gate * gate))
    hidden[...] = (activated * linear).astype(BF)
    cot = hc_own[...] + hc_far[...]
    cots[:, :384] = (cot * linear * slope).astype(BF)
    cots[:, 384:] = (cot * activated).astype(BF)


def activation(own, far, hc_own, hc_far):
    return pl.pallas_call(
        activation_kernel,
        out_shape=[shape(384, 384), shape(384, 768)],
        cost_estimate=pl.CostEstimate(flops=1000, bytes_accessed=1000, transcendentals=0),
        name="activation",
    )(own, far, hc_own, hc_far)


def stack_tokens(idx, own, other, dst):
    dst[rows_of(idx[I_C])] = own[...]
    dst[rows_of(1 - idx[I_C])] = other[...]


def transposed(idx, own, other, dst):
    dst[:, rows_of(idx[I_C])] = own[...].T
    dst[:, rows_of(1 - idx[I_C])] = other[...].T


def weight_grad_kernel(idx, hidden, hidden_far, cots, cots_far, local, remote, *refs):
    pieces = refs[:4]
    out, ht, ct, ds, xs, stage, sems = refs[4:]
    copies = Copies(sems)
    loads = cot_copies(copies, idx, local, remote, ds)
    for piece, step in zip(pieces, STEPS):
        for slot in range(4):
            dst = xs.at[rows_of(token_of(idx, slot)), block(column(idx, step, slot))]
            loads.append(copies.start(piece.at[slot], dst))
    transposed(idx, hidden, hidden_far, ht)
    transposed(idx, cots, cots_far, ct)
    wait(loads)
    leaving = []
    for j in range(ZN):
        columns = slice(256 * j, 256 * j + 256)
        stage[j, :768] = dot(ct[...], xs[:, columns]).astype(BF)
        stage[j, 768:] = dot(ht[...], ds[:, columns]).astype(BF)
        leaving.append(copies.start(stage.at[j], out.at[j]))
    wait(leaving)


def weight_grads(idx, hidden, hidden_far, cots, cots_far, local, remote, x):
    half = pltpu.VMEM((768, 2048), BF)
    scratch = [pltpu.VMEM((384, 768), BF), pltpu.VMEM((768, 768), BF), half, half, pltpu.VMEM((8, 1152, 256), BF)]
    args = (idx, hidden, hidden_far, cots, cots_far, local, remote, *x)
    return call(weight_grad_kernel, shape(8, 1152, 256), scratch, 26, args, "weight_grads", ANY, (1, 2, 3, 4))


def output_kernel(idx, own, other, w, here, up, down, across_up, across_down, hs, os, stage, sems):
    copies = Copies(sems)
    weights = output_weight_copies(copies, w, os)
    stack_tokens(idx, own, other, hs)
    wait(weights)
    leaving = []
    for step, out in ((2, None), (1, up), (3, down), (0, here)):
        for slot in range(4):
            stage[step, slot] = dot(hs[rows_of(token_of(idx, slot))], os[:, block(column(idx, step, slot))]).astype(BF)
        if out is None:
            leaving.append(copies.start(stage.at[step, pl.ds(0, 2)], across_up))
            leaving.append(copies.start(stage.at[step, pl.ds(2, 2)], across_down))
        else:
            leaving.append(copies.start(stage.at[step], out))
    wait(leaving)


def outputs(idx, own, other, w):
    outs = [shape(4, 384, 256)] * 3 + [shape(2, 384, 256)] * 2
    scratch = [pltpu.VMEM((768, 384), BF), pltpu.VMEM((384, 2048), BF), pltpu.VMEM((4, 4, 384, 256), BF)]
    return call(output_kernel, outs, scratch, 13, (idx, own, other, w), "outputs", ANY, (1, 2), 40_000_000)


def input_grad_kernel(idx, own, other, w, first, second, cs, ws, sf, ss, sems):
    copies = Copies(sems)
    weights = [copies.start(w.at[:, pl.ds(256 * p, 256)], ws.at[:, :, 256 * p : 256 * p + 256]) for p in range(3)]
    stack_tokens(idx, own, other, cs)
    wait(weights)
    leaving = []
    for step in range(YN):
        for core in range(2):
            j = column(idx, step, core)
            for pair, (stage, out) in enumerate(((sf, first), (ss, second))):
                stage[core, step] = dot(cs[rows_of(token_of(idx, 2 * pair))], ws[j], 1, 1).astype(BF)
        for stage, out in ((sf, first), (ss, second)):
            leaving.append(copies.start(stage.at[:, step], out.at[:, step]))
    wait(leaving)


def input_grads(idx, own, other, w):
    stage = pltpu.VMEM((2, 4, 384, 256), BF)
    scratch = [pltpu.VMEM((768, 768), BF), pltpu.VMEM((8, 256, 768), BF), stage, stage]
    return call(input_grad_kernel, [shape(2, 4, 384, 256)] * 2, scratch, 19, (idx, own, other, w), "input_grads", ANY, (1, 2))


def pack_kernel(gate, linear, out, packed):
    packed[0:256] = gate[:, 0:256]
    packed[256:512, 0:128] = gate[:, 256:384]
    packed[256:512, 128:256] = linear[:, 0:128]
    packed[512:768] = linear[:, 128:384]
    packed[768:1152] = out[...]


def pack(gate, linear, out):
    return pl.pallas_call(pack_kernel, out_shape=shape(1152, 256), name="pack")(gate, linear, out)


def finish_kernel(share, gate, linear, out):
    gate[...] = share[:384].astype(F32).T
    linear[...] = share[384:768].astype(F32).T
    out[...] = share[768:].astype(F32)


def finish(share):
    outs = [shape(256, 384, dtype=F32), shape(256, 384, dtype=F32), shape(384, 256, dtype=F32)]
    cost = pl.CostEstimate(flops=0, bytes_accessed=50_000_000, transcendentals=0)
    return pl.pallas_call(finish_kernel, out_shape=outs, cost_estimate=cost, name="finish")(share)


def sum_x(first, second):
    from_above = move(first, inverse(X_STEPS[0]))
    from_below = move(second, inverse(X_STEPS[1]))
    from_across = move(second, X_STEPS[2])
    return add(first, from_above, from_below, from_across)


def split(total, is_l):
    return jnp.where(is_l, total[0], move(total[1], inverse(FUSE)))


def per_device(inputs, out_cotangent, gate_weight, linear_weight, output_weight):
    dp, mp = lax.axis_index("dp"), lax.axis_index("mp")
    h, z, l, y, c = dp // 8, dp % 8, mp // 8, (mp // 2) % 4, mp % 2
    is_l = c == l
    ha = jnp.where(is_l | (l == 1), h, 1 - h)
    idx = jnp.stack([z, y, c, h, ha, l]).astype(jnp.int32)

    shard = move(pack(gate_weight, linear_weight, output_weight), WEIGHT)
    mine = jnp.stack([inputs, move(inputs, FUSE)])
    shard, mine = lax.optimization_barrier((shard, mine))
    w = lax.all_gather(shard, "dp", axis_index_groups=Z_GROUPS)
    below, above, across = [move(mine, pairs) for pairs in X_STEPS]
    half = lax.dynamic_slice(out_cotangent, (0, c * 2048), (384, 2048))
    slots = jnp.concatenate([jnp.where(is_l, mine, below), jnp.where(is_l, across, above)])
    slots, half = lax.optimization_barrier((slots, half))
    x = [slots, *[move(slots, pairs) for pairs in Y_STEPS]]
    remote = move(half, ACROSS)

    far, own = projections(idx, x, w)
    idx, far = lax.optimization_barrier((idx, far))
    far = move(far, CORE)
    hc_far, hc_own = hidden_cots(idx, out_cotangent, remote, w)
    hc_far = move(hc_far, CORE)
    hidden, cots = activation(own, far, hc_own, hc_far)
    hidden_far = move(hidden, CORE)
    cots_far = move(cots, CORE)

    parts = weight_grads(idx, hidden, hidden_far, cots, cots_far, out_cotangent, remote, x)
    idx, parts = lax.optimization_barrier((idx, parts))
    share = lax.psum_scatter(parts.reshape(8 * 1152, 256), "dp", scatter_dimension=0, axis_index_groups=Z_GROUPS, tiled=True)
    first, second = input_grads(idx, cots, cots_far, w)
    idx, first, second = lax.optimization_barrier((idx, first, second))
    here, up, down, across_up, across_down = outputs(idx, hidden, hidden_far, w)

    zero = jnp.zeros((), BF)
    up = add(up, lax.pad(move(across_up, Y_STEPS[0]), zero, ((0, 2, 0), (0, 0, 0), (0, 0, 0))))
    down = add(down, lax.pad(move(across_down, Y_STEPS[1]), zero, ((2, 0, 0), (0, 0, 0), (0, 0, 0))))
    sums = add(here, move(up, Y_STEPS[0]), move(down, Y_STEPS[1]))

    layer_output = split(sum_x(sums[:2], sums[2:]), is_l)

    total = sum_x(first, second)
    total, share = lax.optimization_barrier((total, share))
    gate_grad, linear_grad, output_grad = finish(move(share, inverse(WEIGHT)))
    rows = split(total, is_l)
    input_grad = add(rows[0], move(rows[1], Y_STEPS[0]), move(rows[3], Y_STEPS[1]), move(rows[2], Y_STEPS[2]))
    return (layer_output, input_grad, gate_grad, linear_grad, output_grad)


def solution(mesh):
    return jax.shard_map(
        per_device,
        mesh=mesh,
        in_specs=(P("dp", "mp"), P("dp", None), P("dp", "mp"), P("dp", "mp"), P("mp", "dp")),
        out_specs=(P("dp", "mp"), P("dp", "mp"), P("dp", "mp"), P("dp", "mp"), P("mp", "dp")),
        check_vma=False,
    )
```
